32 devices in a mesh: dp: 4 (over z), expert: 8 (over y, x, core).
Axes of the slice: x: 2, y: 2, z: 4, core: 2. Of those that a mesh axis runs over, the one named last changes fastest.
Arguments:
- tokens: bfloat16 [4096, 2048], P(('dp', 'expert')), may hold values from -6 to 6
- grad_mixed: bfloat16 [4096, 2048], P(('dp', 'expert')), may hold values from -0.059814453 to 0.059814453
- expert_ids: int32 [4096, 8], P(('dp', 'expert')), may hold values from 0 to 15, all different within a row; in each aligned block of 128 rows (0 to 127, 128 to 255, ...) at most 128 rows name the same one
- gate_probs: bfloat16 [4096, 8], P(('dp', 'expert')), may hold values from 0.019897461 to 0.25
- gate_proj: bfloat16 [16, 2048, 768], P('expert'), may hold values from -0.125 to 0.125
- up_proj: bfloat16 [16, 2048, 768], P('expert'), may hold values from -0.125 to 0.125
- down_proj: bfloat16 [16, 768, 2048], P('expert'), may hold values from -0.21875 to 0.21875
- share_down: float32 [4, 4, 4], replicated, may hold values from -3 to 3
- share_up: float32 [4, 4, 4], replicated, may hold values from -3 to 3
- factor_down: float32 [16, 4, 512, 16], P('expert'), may hold values from -0.125 to 0.125
- factor_up: float32 [16, 4, 16, 192], P('expert'), may hold values from -0.5 to 0.5
Outputs:
- mixed: bfloat16 [4096, 2048], P(('dp', 'expert'))
- grad_factor_down: float32 [16, 4, 512, 16], P('expert')
- grad_factor_up: float32 [16, 4, 16, 192], P('expert')
- grad_share_down: float32 [4, 4, 4], replicated
- grad_share_up: float32 [4, 4, 4], replicated
The draws below stay inside these ranges and needn't reach their ends.
Inputs may be any that keep to these rules, and one draw needn't show every extreme that they name: `expert_ids`: each row names 8 different experts. In the rows of one device (aligned blocks of 128 rows) no expert is named more than 128 times, a bound that some block reaches.
All inputs are finite; a program needn't handle non-finite values.
Results may differ from the reference program's by a relative error of at most 0.0096.
Values may be sent and summed in bfloat16 or wider, within the bound.
A program may use at most 192 MiB of HBM per device.

```python
import math
from functools import partial
import jax
import jax.numpy as jnp
import numpy as np
from jax import lax

D = 2048
FF = 768
RANK = 64
KRON = 4
TOP = 8
TOK_DEV = 128
EXPERTS = 16
CAP = 128
TOKENS = 4096
N_DP = 4
N_EXPERT = 8


def block_scale(key, shape, cuts, least, top_value):
    def one(dim, shards_of):
        draws = jax.random.uniform(jax.random.fold_in(jax.random.fold_in(key, 6), dim), (shards_of,), jnp.float32, least / len(cuts), top_value / len(cuts))
        return jnp.repeat(jnp.exp(draws), shape[dim] // shards_of).reshape((-1,) + (1,) * (len(shape) - dim - 1))

    factor_of = one(*cuts[0])
    for cut in cuts[1:]:
        factor_of = factor_of * one(*cut)
    return factor_of


def shared_out(rng, own, number, rows, count, top, bound, slope):
    ranking = jax.random.permutation(rng, count)
    crowded, usual = load_shares(count, rows * top, bound, slope, True), load_shares(count, rows * top, bound, slope, False)
    places = jnp.arange(count)

    def named(tallies, rotation):
        used = int((tallies > 0).sum())
        fixed = max(1, used // 4)
        shifted = fixed + (places - fixed + rotation * (used - fixed)) % max(1, count - fixed)
        return jnp.zeros((count,), jnp.int32).at[ranking[jnp.where(places < fixed, places, shifted)]].set(jnp.asarray(tallies, jnp.int32))

    tallies = jnp.where(number % 4 == 0, named(crowded, number // 4), named(usual, number - number // 4 - 1))
    mixed = jax.random.permutation(jax.random.fold_in(own, 3), count)
    donor, taker = mixed[0:count // 2 * 2:2], mixed[1:count // 2 * 2:2]
    margin = jnp.minimum(tallies[donor] - 1, bound - tallies[taker]) // 2
    margin = jnp.where((donor == ranking[0]) | (taker == ranking[0]) | (tallies[taker] == 0), 0, jnp.maximum(margin, 0))
    shifted = jax.random.randint(jax.random.fold_in(own, 4), (count // 2,), 0, 1 << 20) % (margin + 1)
    tallies = tallies.at[donor].add(-shifted).at[taker].add(shifted)
    labels = jnp.searchsorted(jnp.cumsum(tallies), jnp.arange(rows * top), side="right").astype(jnp.int32)
    listing = labels.reshape(top, rows).T
    listing = listing[jax.random.permutation(jax.random.fold_in(own, 1), rows)]
    rotation = jax.random.randint(jax.random.fold_in(own, 2), (rows, 1), 0, top)
    return jnp.take_along_axis(listing, (jnp.arange(top)[None, :] + rotation) % top, axis=1)


def load_shares(amount, total, limit, slope, full):
    loads = [(1 << 20) // math.isqrt(rank ** slope) + 1 for rank in range(1, amount + 1)]
    largest = limit if full else min(limit, max(-(-total // amount), total * loads[0] // sum(loads)))
    least = 1 if total - largest >= amount - 1 else 0
    given, surplus = [largest] + [least] * (amount - 1), total - largest - least * (amount - 1)
    while surplus > 0:
        free = [i for i in range(1, amount) if given[i] < largest] or [i for i in range(1, amount) if given[i] < limit]
        pool, left = sum([loads[i] for i in free]), surplus
        for i in free:
            more = min(limit - given[i], max(1, left * loads[i] // pool), surplus)
            given[i] = given[i] + more
            surplus = surplus - more
    return np.array(given)


def normal_values(own_key, shape, spread, most, pieces=(), kind=jnp.bfloat16):
    gain = block_scale(own_key, shape, pieces, -0.22, 0.18) if pieces else 1.0
    entries = jax.random.normal(own_key, shape, jnp.float32) * spread * gain
    return jnp.minimum(jnp.maximum(entries, -most), most).astype(kind)


def setup_inputs(seed: int = 0) -> dict:
    key_of = jax.random.split(jax.random.key(seed), 12)
    tokens = normal_values(key_of[0], (TOKENS, D), 1.0, 6.0, ((0, 32),))
    grad_mixed = normal_values(key_of[1], (TOKENS, D), 0.01, 0.059814453, ((0, 32),))
    expert_ids_keys = jax.random.split(jax.random.fold_in(key_of[2], 1), TOKENS // TOK_DEV)
    expert_ids_turns = jax.random.permutation(jax.random.fold_in(key_of[2], 3), TOKENS // TOK_DEV)
    expert_ids = jax.vmap(lambda own, number: shared_out(jax.random.fold_in(key_of[2], 2), own, number, TOK_DEV, EXPERTS, TOP, CAP, 2))(expert_ids_keys, expert_ids_turns).reshape((TOKENS, TOP))
    gate_probs = jnp.clip(0.019897461 + 0.23010254 * jax.random.uniform(key_of[3], (TOKENS, TOP), jnp.float32) ** block_scale(key_of[3], (TOKENS, TOP), ((0, 32),), -0.2, 0.2), 0.019897461, 0.25).astype(jnp.bfloat16)
    gate_proj = normal_values(key_of[4], (EXPERTS, D, FF), D ** -0.5, 0.125, ((0, 8),))
    up_proj = normal_values(key_of[5], (EXPERTS, D, FF), D ** -0.5, 0.125, ((0, 8),))
    down_proj = normal_values(key_of[6], (EXPERTS, FF, D), FF ** -0.5, 0.21875, ((0, 8),))
    share_down = normal_values(key_of[7], (KRON, KRON, KRON), 0.5, 3.0, (), jnp.float32)
    share_up = normal_values(key_of[8], (KRON, KRON, KRON), 0.5, 3.0, (), jnp.float32)
    factor_down = normal_values(key_of[9], (EXPERTS, KRON, D // KRON, RANK // KRON), D ** -0.5, 0.125, ((0, 8),), jnp.float32)
    factor_up = normal_values(key_of[10], (EXPERTS, KRON, RANK // KRON, FF // KRON), (2 * RANK) ** -0.5, 0.5, ((0, 8),), jnp.float32)
    return {"tokens": tokens, "grad_mixed": grad_mixed, "expert_ids": expert_ids, "gate_probs": gate_probs, "gate_proj": gate_proj, "up_proj": up_proj, "down_proj": down_proj, "share_down": share_down, "share_up": share_up, "factor_down": factor_down, "factor_up": factor_up}


def slot_table(ids_block, expert_count, capacity):
    flat_ids = ids_block.reshape(-1).astype(jnp.int32)
    slot_count = flat_ids.shape[0]
    onehot = (flat_ids[:, None] == jnp.arange(expert_count, dtype=jnp.int32)[None, :]).astype(jnp.int32)
    rank_in = jnp.sum((jnp.cumsum(onehot, axis=0) - 1) * onehot, axis=1).astype(jnp.int32)
    position = (flat_ids * capacity + rank_in).astype(jnp.int32)
    slot_map = jnp.full((expert_count * capacity,), slot_count, jnp.int32)
    slot_map = slot_map.at[position].set(jnp.arange(slot_count, dtype=jnp.int32))
    return slot_map, position


def expand(factor_a, factor_b):
    kron_n, rows_b, cols_b = factor_b.shape
    blocks = jnp.einsum("iac,ibd->abcd", factor_a, factor_b, precision=lax.Precision.HIGHEST)
    return blocks.reshape(kron_n * rows_b, kron_n * cols_b)


def factor_grads(factor_a, factor_b, grad_w):
    kron_n, rows_b, cols_b = factor_b.shape
    blocks = grad_w.reshape(kron_n, rows_b, kron_n, cols_b)
    grad_b = jnp.einsum("iac,abcd->ibd", factor_a, blocks, precision=lax.Precision.HIGHEST)
    grad_a = jnp.einsum("ibd,abcd->iac", factor_b, blocks, precision=lax.Precision.HIGHEST)
    return grad_b, grad_a


def expert_forward(row_data, gate_mat, up_mat, down_mat, adapter_down, adapter_up):
    lowrank = jnp.dot(row_data, adapter_down, preferred_element_type=jnp.float32).astype(jnp.bfloat16)
    gate_pre = jnp.dot(row_data, gate_mat, preferred_element_type=jnp.float32) + jnp.dot(lowrank, adapter_up, preferred_element_type=jnp.float32)
    up_pre = jnp.dot(row_data, up_mat, preferred_element_type=jnp.float32)
    hidden = (jax.nn.silu(gate_pre) * up_pre).astype(jnp.bfloat16)
    result = jnp.dot(hidden, down_mat, preferred_element_type=jnp.float32).astype(jnp.bfloat16)
    return result, lowrank, gate_pre, up_pre


def expert_backward(row_data, weighted, down_mat, adapter_up, lowrank, gate_pre, up_pre):
    grad_hidden = jnp.dot(weighted, down_mat.T, preferred_element_type=jnp.float32)
    sigmoid_g = jax.nn.sigmoid(gate_pre)
    grad_gate = (grad_hidden * up_pre * sigmoid_g * (1.0 + gate_pre * (1.0 - sigmoid_g))).astype(jnp.bfloat16)
    grad_aup = jnp.dot(lowrank.T, grad_gate, preferred_element_type=jnp.float32)
    grad_low = jnp.dot(grad_gate, adapter_up.T, preferred_element_type=jnp.float32).astype(jnp.bfloat16)
    grad_adown = jnp.dot(row_data.T, grad_low, preferred_element_type=jnp.float32)
    return grad_adown, grad_aup


def reference(tokens, grad_mixed, expert_ids, gate_probs, gate_proj, up_proj, down_proj, share_down, share_up, factor_down, factor_up):
    block_count = N_DP * N_EXPERT
    slot_count = TOK_DEV * TOP
    slot_maps, positions = jax.vmap(partial(slot_table, expert_count=EXPERTS, capacity=CAP))(expert_ids.reshape(block_count, TOK_DEV, TOP))
    by_expert = slot_maps.reshape(block_count, EXPERTS, CAP).transpose(1, 0, 2)
    offsets = jnp.arange(block_count, dtype=jnp.int32)[:, None] * slot_count
    sentinel = block_count * slot_count
    zero_row = jnp.zeros((1, D), tokens.dtype)
    tok_pad = jnp.concatenate([tokens, zero_row], axis=0)
    grad_pad = jnp.concatenate([grad_mixed, zero_row], axis=0)
    gate_pad = jnp.concatenate([gate_probs.reshape(-1), jnp.zeros((1,), gate_probs.dtype)])

    def per_expert(running, inputs):
        mixed_acc, share_acc_down, share_acc_up = running
        expert_slots, gate_mat, up_mat, down_mat, piece_down, piece_up = inputs
        global_slot = jnp.where(expert_slots < slot_count, expert_slots + offsets, sentinel).reshape(-1).astype(jnp.int32)
        token_idx = global_slot // TOP
        row_data = tok_pad[token_idx]
        adapter_down = expand(share_down, piece_down).astype(jnp.bfloat16)
        adapter_up = expand(share_up, piece_up).astype(jnp.bfloat16)
        result, lowrank, gate_pre, up_pre = expert_forward(row_data, gate_mat, up_mat, down_mat, adapter_down, adapter_up)
        weight_of = gate_pad[global_slot].astype(jnp.float32)
        mixed_acc = mixed_acc.at[token_idx].add(weight_of[:, None] * result.astype(jnp.float32))
        weighted = (weight_of[:, None] * grad_pad[token_idx].astype(jnp.float32)).astype(jnp.bfloat16)
        grad_adown, grad_aup = expert_backward(row_data, weighted, down_mat, adapter_up, lowrank, gate_pre, up_pre)
        bdown_grad, adown_grad = factor_grads(share_down, piece_down, grad_adown)
        bup_grad, aup_grad = factor_grads(share_up, piece_up, grad_aup)
        return (mixed_acc, share_acc_down + adown_grad, share_acc_up + aup_grad), (bdown_grad, bup_grad)

    initial = (jnp.zeros((TOKENS + 1, D), jnp.float32), jnp.zeros(share_down.shape, jnp.float32), jnp.zeros(share_up.shape, jnp.float32))
    finals, stacked = lax.scan(per_expert, initial, (by_expert, gate_proj, up_proj, down_proj, factor_down, factor_up))
    mixed_acc, adown_total, aup_total = finals
    bdown_all, bup_all = stacked
    return mixed_acc[:TOKENS].astype(jnp.bfloat16), bdown_all, bup_all, adown_total, aup_total
```

```python
from functools import partial

import jax
import jax.numpy as jnp
from jax import lax
from jax.experimental import pallas as pl
from jax.experimental.pallas import tpu as pltpu
from jax.sharding import PartitionSpec as P


def routed_slots(ids_block, first_expert, expert_span, capacity):
    flat_ids = ids_block.reshape(-1).astype(jnp.int32)
    slot_count = flat_ids.shape[0]
    local_ids = flat_ids - first_expert
    onehot = local_ids[:, None] == jnp.arange(expert_span, dtype=jnp.int32)[None, :]
    order = jnp.arange(slot_count, dtype=jnp.int32)
    earlier = (order[:, None] > order[None, :]).astype(jnp.bfloat16)
    before = jnp.dot(earlier, onehot.astype(jnp.bfloat16), preferred_element_type=jnp.float32)
    rank_in = jnp.sum(jnp.where(onehot, before, 0.0), axis=1).astype(jnp.int32)
    inside = (local_ids >= 0) & (local_ids < expert_span)
    position = jnp.where(inside, local_ids * capacity + rank_in, -1)
    targets = jnp.arange(expert_span * capacity, dtype=jnp.int32)
    match = position[:, None] == targets[None, :]
    found = jnp.max(jnp.where(match, order[:, None], -1), axis=0)
    slot_map = jnp.where(found < 0, slot_count, found)
    return (slot_map, position)


def expand(factor_a, factor_b):
    kron_n, rows_b, cols_b = factor_b.shape
    blocks = jnp.einsum("iac,ibd->abcd", factor_a, factor_b, precision=lax.Precision.HIGHEST)
    return blocks.reshape(kron_n * rows_b, kron_n * cols_b)


def factor_grads(factor_a, factor_b, grad_w):
    kron_n, rows_b, cols_b = factor_b.shape
    blocks = grad_w.reshape(kron_n, rows_b, kron_n, cols_b)
    grad_b = jnp.einsum("iac,abcd->ibd", factor_a, blocks, precision=lax.Precision.HIGHEST)
    grad_a = jnp.einsum("ibd,abcd->iac", factor_b, blocks, precision=lax.Precision.HIGHEST)
    return (grad_b, grad_a)


def expert_forward(row_data, gate_mat, up_mat, down_mat, adapter_down, adapter_up):
    lowrank = jnp.dot(row_data, adapter_down, preferred_element_type=jnp.float32).astype(
        jnp.bfloat16
    )
    gate_pre = jnp.dot(row_data, gate_mat, preferred_element_type=jnp.float32) + jnp.dot(
        lowrank, adapter_up, preferred_element_type=jnp.float32
    )
    up_pre = jnp.dot(row_data, up_mat, preferred_element_type=jnp.float32)
    hidden = (jax.nn.silu(gate_pre) * up_pre).astype(jnp.bfloat16)
    result = jnp.dot(hidden, down_mat, preferred_element_type=jnp.float32).astype(jnp.bfloat16)
    return (result, lowrank, gate_pre, up_pre)


def expert_backward(row_data, weighted, down_mat, adapter_up, lowrank, gate_pre, up_pre):
    grad_hidden = lax.dot_general(
        weighted, down_mat, (((1,), (1,)), ((), ())), preferred_element_type=jnp.float32
    )
    sigmoid_g = jax.nn.sigmoid(gate_pre)
    grad_gate = (grad_hidden * up_pre * sigmoid_g * (1.0 + gate_pre * (1.0 - sigmoid_g))).astype(
        jnp.bfloat16
    )
    grad_aup = lax.dot_general(
        lowrank, grad_gate, (((0,), (0,)), ((), ())), preferred_element_type=jnp.float32
    )
    grad_low = lax.dot_general(
        grad_gate, adapter_up, (((1,), (1,)), ((), ())), preferred_element_type=jnp.float32
    ).astype(jnp.bfloat16)
    grad_adown = lax.dot_general(
        row_data, grad_low, (((0,), (0,)), ((), ())), preferred_element_type=jnp.float32
    )
    return (grad_adown, grad_aup)


def on_device(
    tokens,
    grad_mixed,
    expert_ids,
    gate_probs,
    gate_proj,
    up_proj,
    down_proj,
    share_down,
    share_up,
    factor_down,
    factor_up,
):
    tok_rows, top_k = expert_ids.shape
    slot_count = tok_rows * top_k
    local_experts = gate_proj.shape[0]
    groups = lax.axis_size("expert")
    expert_count = local_experts * groups
    capacity = 2 * slot_count // expert_count
    model_width = tokens.shape[1]
    zero_row = jnp.zeros((1, model_width), tokens.dtype)
    own_map, own_position = routed_slots(expert_ids, 0, expert_count, capacity)
    all_tokens, all_ids = (
        lax.all_gather(tokens, "expert", axis=0, tiled=True),
        lax.all_gather(expert_ids, "expert", axis=0, tiled=True),
    )
    first_local = lax.axis_index("expert") * local_experts
    tables, unused = jax.vmap(
        partial(
            routed_slots, first_expert=first_local, expert_span=local_experts, capacity=capacity
        )
    )(all_ids.reshape(groups, tok_rows, top_k))
    own_slots = tables.reshape(groups, local_experts, capacity).transpose(1, 0, 2)
    source = jnp.arange(groups, dtype=jnp.int32)[None, :, None] * slot_count
    global_slot = jnp.where(own_slots < slot_count, own_slots + source, groups * slot_count)
    padded = jnp.concatenate([all_tokens, zero_row], axis=0)
    received = padded[(global_slot // top_k).reshape(-1)].reshape(
        local_experts, groups * capacity, model_width
    )
    outputs = []
    stashed = []
    for member in range(local_experts):
        adapter_down = expand(share_down, factor_down[member]).astype(jnp.bfloat16)
        adapter_up = expand(share_up, factor_up[member]).astype(jnp.bfloat16)
        result, lowrank, gate_pre, up_pre = expert_forward(
            received[member],
            gate_proj[member],
            up_proj[member],
            down_proj[member],
            adapter_down,
            adapter_up,
        )
        outputs.append(result)
        stashed.append((lowrank, gate_pre, up_pre, adapter_up))
    returned = lax.all_to_all(jnp.stack(outputs), "expert", split_axis=1, concat_axis=0, tiled=True)
    picked = returned.reshape(expert_count * capacity, model_width)[own_position].astype(
        jnp.float32
    )
    mixed = jnp.sum(
        picked.reshape(tok_rows, top_k, model_width) * gate_probs.astype(jnp.float32)[:, :, None],
        axis=1,
    ).astype(jnp.bfloat16)
    gate_pad = jnp.concatenate([gate_probs.reshape(-1), jnp.zeros((1,), gate_probs.dtype)])
    grad_pad = jnp.concatenate([grad_mixed, zero_row], axis=0)
    weighted = (
        gate_pad[own_map].astype(jnp.float32)[:, None]
        * grad_pad[own_map // top_k].astype(jnp.float32)
    ).astype(jnp.bfloat16)
    grad_slots = lax.all_to_all(
        weighted.reshape(expert_count, capacity, model_width),
        "expert",
        split_axis=0,
        concat_axis=1,
        tiled=True,
    )
    bdown_list = []
    bup_list = []
    adown_total = jnp.zeros(share_down.shape, jnp.float32)
    aup_total = jnp.zeros(share_up.shape, jnp.float32)
    for member in range(local_experts):
        lowrank, gate_pre, up_pre, adapter_up = stashed[member]
        grad_adown, grad_aup = expert_backward(
            received[member],
            grad_slots[member],
            down_proj[member],
            adapter_up,
            lowrank,
            gate_pre,
            up_pre,
        )
        bdown_grad, adown_grad = factor_grads(share_down, factor_down[member], grad_adown)
        bup_grad, aup_grad = factor_grads(share_up, factor_up[member], grad_aup)
        bdown_list.append(bdown_grad)
        bup_list.append(bup_grad)
        adown_total = adown_total + adown_grad
        aup_total = aup_total + aup_grad
    bdown_all = jnp.stack(bdown_list)
    bup_all = jnp.stack(bup_list)
    bdown_all, bup_all, adown_total, aup_total = lax.psum(
        (bdown_all, bup_all, adown_total, aup_total), "dp"
    )
    adown_total, aup_total = lax.psum((adown_total, aup_total), "expert")
    return (mixed, bdown_all, bup_all, adown_total, aup_total)


def group_kernel(
    tok_ref, grad_ref, ids_ref, probs_ref, adt_ref, aup_ref, gate_hbm, up_hbm, down_hbm,
    mixed_ref, gat_ref, gb_ref,
    xs, gs, gate_v, up_v, down_v, coef, low_v, hid, part, twin_in, mixed_in,
    w_sem, tok_send, tok_recv, gr_send, gr_recv, tw_send, tw_recv, mx_send, mx_recv,
):
    f32, bf16 = jnp.float32, jnp.bfloat16
    rows, width = tok_ref.shape
    ff = gate_v.shape[2]
    chunk = 256
    me = lax.axis_index("expert")
    core = me % 2
    other = 1 - core
    xpos = (me // 2) % 2
    ypos = me // 4
    twin = me + 1 - 2 * core
    x_dev = me + 2 - 4 * xpos
    y_dev = me + 4 - 8 * ypos
    d_dev = x_dev + 4 - 8 * ypos
    peers = (twin, x_dev, y_dev, d_dev)

    loads = [
        pltpu.make_async_copy(gate_hbm, gate_v, w_sem.at[0]),
        pltpu.make_async_copy(up_hbm, up_v, w_sem.at[1]),
        pltpu.make_async_copy(down_hbm, down_v, w_sem.at[2]),
    ]
    for load in loads:
        load.start()
    barrier = pltpu.get_barrier_semaphore()
    for peer in peers:
        pl.semaphore_signal(
            barrier, inc=1, device_id={"expert": peer}, device_id_type=pl.DeviceIdType.MESH
        )

    lanes = lax.broadcasted_iota(jnp.int32, (rows, 128), 1)
    weights = jnp.zeros((rows, 128), f32)
    for k in range(ids_ref.shape[1]):
        weights = weights + jnp.where(
            ids_ref[:, k : k + 1] == lanes, probs_ref[:, k : k + 1].astype(f32), 0.0
        )
    xs[0, core, :, :width] = tok_ref[...]
    xs[0, core, :, width:] = weights.astype(bf16)
    gs[0, core] = grad_ref[...]
    pl.semaphore_wait(barrier, len(peers))

    def remote(src, dst, send, recv, device):
        return pltpu.make_async_remote_copy(
            src_ref=src, dst_ref=dst, send_sem=send, recv_sem=recv,
            device_id={"expert": device}, device_id_type=pl.DeviceIdType.MESH,
        )

    def gather_copies(buf, send, recv, via_x):
        pick = lambda slot, to, n: remote(
            buf.at[slot[0], core], buf.at[slot[1], core], send.at[n], recv.at[n], to
        )
        copies = [pick((r, r), twin, r) for r in range(4)]
        copies.append(pick((0, 1), x_dev, 4))
        copies.append(pick((0, 2), y_dev, 5))
        copies.append(pick((1, 3), y_dev, 6) if via_x else pick((2, 3), x_dev, 6))
        return copies

    tok = gather_copies(xs, tok_send, tok_recv, True)
    grd = gather_copies(gs, gr_send, gr_recv, False)
    pair = [
        remote(part.at[r, other], twin_in.at[r], tw_send.at[r], tw_recv.at[r], twin)
        for r in range(4)
    ]
    back = [
        remote(part.at[r, core], mixed_in.at[r], mx_send.at[r], mx_recv.at[r], dev)
        for r, dev in ((1, x_dev), (2, y_dev), (3, d_dev))
    ]

    nt = (((1,), (1,)), ((), ()))

    def forward(r):
        x = lambda: xs[r, :, :, :width].reshape(2 * rows, width)
        low_v[r] = lax.dot_general(x(), adt_ref[...], nt, preferred_element_type=f32).astype(bf16)
        table = xs[r, :, :, width:].reshape(2 * rows, 128).astype(f32)
        at = lax.broadcasted_iota(jnp.int32, (2 * rows, 128), 1)
        for e in range(2):
            weight = jnp.sum(jnp.where(at == 2 * me + e, table, 0.0), axis=1, keepdims=True)

            def step(c, carry):
                here = pl.ds(pl.multiple_of(c * chunk, chunk), chunk)
                wide = pl.ds(pl.multiple_of(e * ff + c * chunk, chunk), chunk)
                gate = jnp.dot(x(), gate_v[e, :, here], preferred_element_type=f32)
                gate = gate + jnp.dot(low_v[r], aup_ref[:, wide], preferred_element_type=f32)
                up = jnp.dot(x(), up_v[e, :, here], preferred_element_type=f32)
                sig = 1.0 / (1.0 + jnp.exp(-gate))
                scaled = weight * up * sig
                hid[:, wide] = (scaled * gate).astype(bf16)
                coef[r, :, wide] = scaled * (1.0 + gate * (1.0 - sig))
                return carry

            lax.fori_loop(0, ff // chunk, step, 0)

        def out_step(c, carry):
            here = pl.ds(pl.multiple_of(c * chunk, chunk), chunk)
            out = jnp.dot(hid[...], down_v[:, here], preferred_element_type=f32)
            part[r, :, :, here] = out.astype(bf16).reshape(2, rows, chunk)
            return carry

        lax.fori_loop(0, width // chunk, out_step, 0)

    def backward(r):
        def step(c, carry):
            here = pl.ds(pl.multiple_of(c * chunk, chunk), chunk)
            grad = lax.dot_general(
                gs[r].reshape(2 * rows, width), down_v[here, :], nt, preferred_element_type=f32
            )
            hid[:, here] = (grad * coef[r, :, here]).astype(bf16)
            return carry

        lax.fori_loop(0, 2 * ff // chunk, step, 0)
        low_grad = lax.dot_general(hid[...], aup_ref[...], nt, preferred_element_type=f32)
        low_grad_t = low_grad.T.astype(bf16)
        low_t = low_v[r].astype(f32).T.astype(bf16)
        up_part = jnp.dot(low_t, hid[...], preferred_element_type=f32)
        down_part = jnp.dot(
            low_grad_t, xs[r, :, :, :width].reshape(2 * rows, width), preferred_element_type=f32
        )
        if r == 0:
            gb_ref[...] = up_part
            gat_ref[...] = down_part
        else:
            gb_ref[...] += up_part
            gat_ref[...] += down_part

    def combine(r):
        pair[r].wait()
        part[r, core] = (part[r, core].astype(f32) + twin_in[r].astype(f32)).astype(bf16)
        if r:
            back[r - 1].start()

    for n in (4, 5, 0):
        tok[n].start()
    for load in loads[:2]:
        load.wait()
    tok[0].wait_recv()
    loads[2].wait()
    forward(0)
    pair[0].start()
    tok[4].wait_recv()
    tok[6].start()
    tok[1].start()
    tok[5].wait_recv()
    tok[2].start()
    for n in (5, 4, 0):
        grd[n].start()
    tok[1].wait_recv()
    forward(1)
    pair[1].start()
    tok[6].wait_recv()
    tok[3].start()
    tok[2].wait_recv()
    forward(2)
    pair[2].start()
    combine(1)
    grd[5].wait_recv()
    grd[6].start()
    grd[2].start()
    tok[3].wait_recv()
    forward(3)
    pair[3].start()
    combine(2)
    grd[4].wait_recv()
    grd[1].start()
    grd[0].wait_recv()
    backward(0)
    combine(3)
    combine(0)
    grd[6].wait_recv()
    grd[3].start()
    grd[1].wait_recv()
    backward(1)
    grd[2].wait_recv()
    backward(2)
    grd[3].wait_recv()
    backward(3)
    total = part[0, core].astype(f32)
    for n in range(3):
        back[n].wait()
        total = total + mixed_in[n + 1].astype(f32)
    mixed_ref[...] = total.astype(bf16)
    for copy in tok + grd:
        copy.wait_send()


def fused_device(
    tokens, grad_mixed, expert_ids, gate_probs, gate_proj, up_proj, down_proj,
    share_down, share_up, factor_down, factor_up,
):
    f32, bf16 = jnp.float32, jnp.bfloat16
    rows, width = tokens.shape
    members, ff = gate_proj.shape[0], gate_proj.shape[2]
    high = lax.Precision.HIGHEST
    adt = jnp.einsum("iac,eibd->ecdab", share_down, factor_down, precision=high)
    adt = adt.reshape(-1, width).astype(bf16)
    rank = adt.shape[0] // members
    ups = jnp.einsum("iac,eibd->eabcd", share_up, factor_up, precision=high)
    ups = ups.reshape(members, rank, ff).astype(bf16)
    aup = jnp.zeros((members * rank, members * ff), bf16)
    for e in range(members):
        aup = aup.at[e * rank : (e + 1) * rank, e * ff : (e + 1) * ff].set(ups[e])
    vmem = pl.BlockSpec(memory_space=pltpu.VMEM)
    hbm = pl.BlockSpec(memory_space=pl.ANY)
    dma = pltpu.SemaphoreType.DMA
    pairs = members * 4 * 2 * rows
    mixed, gat, gb = pl.pallas_call(
        group_kernel,
        out_shape=(
            jax.ShapeDtypeStruct((rows, width), bf16),
            jax.ShapeDtypeStruct((members * rank, width), f32),
            jax.ShapeDtypeStruct((members * rank, members * ff), f32),
        ),
        in_specs=[vmem] * 6 + [hbm] * 3,
        out_specs=(vmem, vmem, vmem),
        scratch_shapes=[
            pltpu.VMEM((4, 2, rows, width + 128), bf16),
            pltpu.VMEM((4, 2, rows, width), bf16),
            pltpu.VMEM((members, width, ff), bf16),
            pltpu.VMEM((members, width, ff), bf16),
            pltpu.VMEM((members * ff, width), bf16),
            pltpu.VMEM((4, 2 * rows, members * ff), f32),
            pltpu.VMEM((4, 2 * rows, members * rank), bf16),
            pltpu.VMEM((2 * rows, members * ff), bf16),
            pltpu.VMEM((4, 2, rows, width), bf16),
            pltpu.VMEM((4, rows, width), bf16),
            pltpu.VMEM((4, rows, width), bf16),
            dma((3,)), dma((7,)), dma((7,)), dma((7,)), dma((7,)),
            dma((4,)), dma((4,)), dma((4,)), dma((4,)),
        ],
        compiler_params=pltpu.CompilerParams(
            collective_id=0, has_side_effects=True, vmem_limit_bytes=58 * 1024 * 1024
        ),
        cost_estimate=pl.CostEstimate(
            flops=8 * pairs * width * ff, bytes_accessed=6 * members * width * ff,
            transcendentals=pairs * ff,
        ),
    )(
        tokens, grad_mixed, expert_ids, gate_probs, adt, aup,
        gate_proj, up_proj, down_proj.reshape(members * ff, width),
    )
    return finish(mixed, gat, gb, share_down, share_up, factor_down, factor_up)


def finish(mixed, gat, gb, share_down, share_up, factor_down, factor_up):
    high = lax.Precision.HIGHEST
    members, kron_n, rows_d, cols_d = factor_down.shape
    rows_u, cols_u = factor_up.shape[2:]
    rank, ff = kron_n * rows_u, kron_n * cols_u
    blocks_d = gat.reshape(members, kron_n, cols_d, kron_n, rows_d)
    blocks_u = jnp.stack(
        [gb[e * rank : (e + 1) * rank, e * ff : (e + 1) * ff] for e in range(members)]
    ).reshape(members, kron_n, rows_u, kron_n, cols_u)
    bd = jnp.einsum("iac,ecdab->eibd", share_down, blocks_d, precision=high)
    sd = jnp.einsum("eibd,ecdab->iac", factor_down, blocks_d, precision=high)
    bu = jnp.einsum("iac,eabcd->eibd", share_up, blocks_u, precision=high)
    su = jnp.einsum("eibd,eabcd->iac", factor_up, blocks_u, precision=high)
    flat = jnp.concatenate([v.reshape(-1) for v in (bd, bu)])
    flat = lax.psum(flat, "dp")
    small = lax.psum(jnp.stack([sd, su]), ("dp", "expert"))
    bd_all = flat[: bd.size].reshape(bd.shape)
    bu_all = flat[bd.size :].reshape(bu.shape)
    return (mixed, bd_all, bu_all, small[0], small[1])


def solution(mesh):
    body = fused_device if mesh.shape["expert"] == 8 else on_device
    return jax.shard_map(
        body,
        mesh=mesh,
        in_specs=(
            P(("dp", "expert"), None),
            P(("dp", "expert"), None),
            P(("dp", "expert"), None),
            P(("dp", "expert"), None),
            P("expert", None, None),
            P("expert", None, None),
            P("expert", None, None),
            P(),
            P(),
            P("expert", None, None, None),
            P("expert", None, None, None),
        ),
        out_specs=(
            P(("dp", "expert"), None),
            P("expert", None, None, None),
            P("expert", None, None, None),
            P(),
            P(),
        ),
        check_vma=False,
    )
```

```python
from functools import partial

import jax
import jax.numpy as jnp
from jax import lax
from jax.experimental import pallas as pl
from jax.experimental.pallas import tpu as pltpu
from jax.sharding import PartitionSpec as P


def routed_slots(ids_block, first_expert, expert_span, capacity):
    flat_ids = ids_block.reshape(-1).astype(jnp.int32)
    slot_count = flat_ids.shape[0]
    local_ids = flat_ids - first_expert
    onehot = local_ids[:, None] == jnp.arange(expert_span, dtype=jnp.int32)[None, :]
    order = jnp.arange(slot_count, dtype=jnp.int32)
    earlier = (order[:, None] > order[None, :]).astype(jnp.bfloat16)
    before = jnp.dot(earlier, onehot.astype(jnp.bfloat16), preferred_element_type=jnp.float32)
    rank_in = jnp.sum(jnp.where(onehot, before, 0.0), axis=1).astype(jnp.int32)
    inside = (local_ids >= 0) & (local_ids < expert_span)
    position = jnp.where(inside, local_ids * capacity + rank_in, -1)
    targets = jnp.arange(expert_span * capacity, dtype=jnp.int32)
    match = position[:, None] == targets[None, :]
    found = jnp.max(jnp.where(match, order[:, None], -1), axis=0)
    slot_map = jnp.where(found < 0, slot_count, found)
    return (slot_map, position)


def expand(factor_a, factor_b):
    kron_n, rows_b, cols_b = factor_b.shape
    blocks = jnp.einsum("iac,ibd->abcd", factor_a, factor_b, precision=lax.Precision.HIGHEST)
    return blocks.reshape(kron_n * rows_b, kron_n * cols_b)


def factor_grads(factor_a, factor_b, grad_w):
    kron_n, rows_b, cols_b = factor_b.shape
    blocks = grad_w.reshape(kron_n, rows_b, kron_n, cols_b)
    grad_b = jnp.einsum("iac,abcd->ibd", factor_a, blocks, precision=lax.Precision.HIGHEST)
    grad_a = jnp.einsum("ibd,abcd->iac", factor_b, blocks, precision=lax.Precision.HIGHEST)
    return (grad_b, grad_a)


def expert_forward(row_data, gate_mat, up_mat, down_mat, adapter_down, adapter_up):
    lowrank = jnp.dot(row_data, adapter_down, preferred_element_type=jnp.float32).astype(
        jnp.bfloat16
    )
    gate_pre = jnp.dot(row_data, gate_mat, preferred_element_type=jnp.float32) + jnp.dot(
        lowrank, adapter_up, preferred_element_type=jnp.float32
    )
    up_pre = jnp.dot(row_data, up_mat, preferred_element_type=jnp.float32)
    hidden = (jax.nn.silu(gate_pre) * up_pre).astype(jnp.bfloat16)
    result = jnp.dot(hidden, down_mat, preferred_element_type=jnp.float32).astype(jnp.bfloat16)
    return (result, lowrank, gate_pre, up_pre)


def expert_backward(row_data, weighted, down_mat, adapter_up, lowrank, gate_pre, up_pre):
    grad_hidden = lax.dot_general(
        weighted, down_mat, (((1,), (1,)), ((), ())), preferred_element_type=jnp.float32
    )
    sigmoid_g = jax.nn.sigmoid(gate_pre)
    grad_gate = (grad_hidden * up_pre * sigmoid_g * (1.0 + gate_pre * (1.0 - sigmoid_g))).astype(
        jnp.bfloat16
    )
    grad_aup = lax.dot_general(
        lowrank, grad_gate, (((0,), (0,)), ((), ())), preferred_element_type=jnp.float32
    )
    grad_low = lax.dot_general(
        grad_gate, adapter_up, (((1,), (1,)), ((), ())), preferred_element_type=jnp.float32
    ).astype(jnp.bfloat16)
    grad_adown = lax.dot_general(
        row_data, grad_low, (((0,), (0,)), ((), ())), preferred_element_type=jnp.float32
    )
    return (grad_adown, grad_aup)


def on_device(
    tokens,
    grad_mixed,
    expert_ids,
    gate_probs,
    gate_proj,
    up_proj,
    down_proj,
    share_down,
    share_up,
    factor_down,
    factor_up,
):
    tok_rows, top_k = expert_ids.shape
    slot_count = tok_rows * top_k
    local_experts = gate_proj.shape[0]
    groups = lax.axis_size("expert")
    expert_count = local_experts * groups
    capacity = 2 * slot_count // expert_count
    model_width = tokens.shape[1]
    zero_row = jnp.zeros((1, model_width), tokens.dtype)
    own_map, own_position = routed_slots(expert_ids, 0, expert_count, capacity)
    all_tokens, all_ids = (
        lax.all_gather(tokens, "expert", axis=0, tiled=True),
        lax.all_gather(expert_ids, "expert", axis=0, tiled=True),
    )
    first_local = lax.axis_index("expert") * local_experts
    tables, unused = jax.vmap(
        partial(
            routed_slots, first_expert=first_local, expert_span=local_experts, capacity=capacity
        )
    )(all_ids.reshape(groups, tok_rows, top_k))
    own_slots = tables.reshape(groups, local_experts, capacity).transpose(1, 0, 2)
    source = jnp.arange(groups, dtype=jnp.int32)[None, :, None] * slot_count
    global_slot = jnp.where(own_slots < slot_count, own_slots + source, groups * slot_count)
    padded = jnp.concatenate([all_tokens, zero_row], axis=0)
    received = padded[(global_slot // top_k).reshape(-1)].reshape(
        local_experts, groups * capacity, model_width
    )
    outputs = []
    stashed = []
    for member in range(local_experts):
        adapter_down = expand(share_down, factor_down[member]).astype(jnp.bfloat16)
        adapter_up = expand(share_up, factor_up[member]).astype(jnp.bfloat16)
        result, lowrank, gate_pre, up_pre = expert_forward(
            received[member],
            gate_proj[member],
            up_proj[member],
            down_proj[member],
            adapter_down,
            adapter_up,
        )
        outputs.append(result)
        stashed.append((lowrank, gate_pre, up_pre, adapter_up))
    returned = lax.all_to_all(jnp.stack(outputs), "expert", split_axis=1, concat_axis=0, tiled=True)
    picked = returned.reshape(expert_count * capacity, model_width)[own_position].astype(
        jnp.float32
    )
    mixed = jnp.sum(
        picked.reshape(tok_rows, top_k, model_width) * gate_probs.astype(jnp.float32)[:, :, None],
        axis=1,
    ).astype(jnp.bfloat16)
    gate_pad = jnp.concatenate([gate_probs.reshape(-1), jnp.zeros((1,), gate_probs.dtype)])
    grad_pad = jnp.concatenate([grad_mixed, zero_row], axis=0)
    weighted = (
        gate_pad[own_map].astype(jnp.float32)[:, None]
        * grad_pad[own_map // top_k].astype(jnp.float32)
    ).astype(jnp.bfloat16)
    grad_slots = lax.all_to_all(
        weighted.reshape(expert_count, capacity, model_width),
        "expert",
        split_axis=0,
        concat_axis=1,
        tiled=True,
    )
    bdown_list = []
    bup_list = []
    adown_total = jnp.zeros(share_down.shape, jnp.float32)
    aup_total = jnp.zeros(share_up.shape, jnp.float32)
    for member in range(local_experts):
        lowrank, gate_pre, up_pre, adapter_up = stashed[member]
        grad_adown, grad_aup = expert_backward(
            received[member],
            grad_slots[member],
            down_proj[member],
            adapter_up,
            lowrank,
            gate_pre,
            up_pre,
        )
        bdown_grad, adown_grad = factor_grads(share_down, factor_down[member], grad_adown)
        bup_grad, aup_grad = factor_grads(share_up, factor_up[member], grad_aup)
        bdown_list.append(bdown_grad)
        bup_list.append(bup_grad)
        adown_total = adown_total + adown_grad
        aup_total = aup_total + aup_grad
    bdown_all = jnp.stack(bdown_list)
    bup_all = jnp.stack(bup_list)
    bdown_all, bup_all, adown_total, aup_total = lax.psum(
        (bdown_all, bup_all, adown_total, aup_total), "dp"
    )
    adown_total, aup_total = lax.psum((adown_total, aup_total), "expert")
    return (mixed, bdown_all, bup_all, adown_total, aup_total)


def group_kernel(
    sd_ref, su_ref, tok_ref, grad_ref, ids_ref, probs_ref, fd_ref, fu_ref, gate_hbm, up_hbm, down_hbm,
    mixed_ref, fdown_ref, fup_ref, share_ref,
    adt_ref, aup_ref, gat_ref, gb_ref, terms, share_parts, share_in, share_hop, scat_out, scat_in, whole,
    xs, gs, gate_v, up_v, down_v, coef, low_v, hid, part, twin_in, mixed_in,
    w_sem, tok_send, tok_recv, gr_send, gr_recv, tw_send, tw_recv, mx_send, mx_recv,
    sc_send, sc_recv, ga_send, ga_recv, sh_send, sh_recv, hop_send, hop_recv,
):
    f32, bf16 = jnp.float32, jnp.bfloat16
    rows, width = tok_ref.shape
    ff = gate_v.shape[2]
    chunk = 256
    me = lax.axis_index("expert")
    core = me % 2
    other = 1 - core
    xpos = (me // 2) % 2
    ypos = me // 4
    twin = me + 1 - 2 * core
    x_dev = me + 2 - 4 * xpos
    y_dev = me + 4 - 8 * ypos
    d_dev = x_dev + 4 - 8 * ypos
    peers = (twin, x_dev, y_dev, d_dev)
    dp = lax.axis_index("dp")
    n_dp = scat_in.shape[0]
    others = [lax.rem(dp + j, n_dp) for j in range(1, n_dp)]
    kron_n, cols_d, rows_d = fd_ref.shape[1:]
    rows_u, cols_u = fu_ref.shape[2:]
    rank = kron_n * cols_d
    mesh_id = pl.DeviceIdType.MESH

    loads = [
        pltpu.make_async_copy(gate_hbm, gate_v, w_sem.at[0]),
        pltpu.make_async_copy(up_hbm, up_v, w_sem.at[1]),
        pltpu.make_async_copy(down_hbm, down_v, w_sem.at[2]),
    ]
    for load in loads:
        load.start()
    barrier = pltpu.get_barrier_semaphore()
    for peer in peers:
        pl.semaphore_signal(
            barrier, inc=1, device_id={"expert": peer}, device_id_type=mesh_id
        )
    for peer in others:
        pl.semaphore_signal(barrier, inc=1, device_id={"dp": peer}, device_id_type=mesh_id)

    names = lax.broadcasted_iota(jnp.int32, (128, rows), 0)
    probs = probs_ref[...].astype(f32)
    weights = jnp.zeros((128, rows), f32)
    for k in range(ids_ref.shape[0]):
        weights = weights + jnp.where(ids_ref[k : k + 1, :] == names, probs[k : k + 1, :], 0.0)
    weights = weights.T
    xs[0, core, :, :width] = tok_ref[...]
    xs[0, core, :, width:] = weights.astype(bf16)
    gs[0, core] = grad_ref[...]
    pl.semaphore_wait(barrier, len(peers) + len(others))

    def remote(src, dst, send, recv, device, axis="expert"):
        return pltpu.make_async_remote_copy(
            src_ref=src, dst_ref=dst, send_sem=send, recv_sem=recv,
            device_id={axis: device}, device_id_type=mesh_id,
        )

    def gather_copies(buf, send, recv):
        pick = lambda slot, to, n: remote(
            buf.at[slot[0], core], buf.at[slot[1], core], send.at[n], recv.at[n], to
        )
        copies = [pick((r, r), twin, r) for r in range(4)]
        copies.append(pick((0, 1), x_dev, 4))
        copies.append(pick((0, 2), y_dev, 5))
        for n, near, dev in ((6, 1, y_dev), (7, 2, x_dev)):
            span = pl.ds((n - 6) * (rows // 2), rows // 2)
            copies.append(
                remote(
                    buf.at[near, core, span], buf.at[3, core, span], send.at[n], recv.at[n], dev
                )
            )
        return copies

    tok = gather_copies(xs, tok_send, tok_recv)
    grd = gather_copies(gs, gr_send, gr_recv)
    pair = [
        remote(part.at[r, other], twin_in.at[r], tw_send.at[r], tw_recv.at[r], twin)
        for r in range(4)
    ]
    back = [
        remote(part.at[r, core], mixed_in.at[r], mx_send.at[r], mx_recv.at[r], dev)
        for r, dev in ((1, x_dev), (2, y_dev), (3, d_dev))
    ]

    nt = (((1,), (1,)), ((), ()))

    def forward(r):
        x = lambda: xs[r, :, :, :width].reshape(2 * rows, width)
        low_v[r] = lax.dot_general(x(), adt_ref[...], nt, preferred_element_type=f32).astype(bf16)
        table = xs[r, :, :, width:].reshape(2 * rows, 128).astype(f32)
        at = lax.broadcasted_iota(jnp.int32, (2 * rows, 128), 1)
        for e in range(2):
            weight = jnp.sum(jnp.where(at == 2 * me + e, table, 0.0), axis=1, keepdims=True)

            def step(c, carry):
                here = pl.ds(pl.multiple_of(c * chunk, chunk), chunk)
                wide = pl.ds(pl.multiple_of(e * ff + c * chunk, chunk), chunk)
                gate = jnp.dot(x(), gate_v[e, :, here], preferred_element_type=f32)
                gate = gate + jnp.dot(low_v[r], aup_ref[:, wide], preferred_element_type=f32)
                up = jnp.dot(x(), up_v[e, :, here], preferred_element_type=f32)
                sig = 1.0 / (1.0 + jnp.exp(-gate))
                scaled = weight * up * sig
                hid[:, wide] = (scaled * gate).astype(bf16)
                coef[r, :, wide] = scaled * (1.0 + gate * (1.0 - sig))
                return carry

            lax.fori_loop(0, ff // chunk, step, 0)

        def out_step(c, carry):
            here = pl.ds(pl.multiple_of(c * chunk, chunk), chunk)
            out = jnp.dot(hid[...], down_v[:, here], preferred_element_type=f32)
            part[r, :, :, here] = out.astype(bf16).reshape(2, rows, chunk)
            return carry

        lax.fori_loop(0, width // chunk, out_step, 0)

    def backward(r):
        def step(c, carry):
            here = pl.ds(pl.multiple_of(c * chunk, chunk), chunk)
            grad = lax.dot_general(
                gs[r].reshape(2 * rows, width), down_v[here, :], nt, preferred_element_type=f32
            )
            hid[:, here] = (grad * coef[r, :, here]).astype(bf16)
            return carry

        lax.fori_loop(0, 2 * ff // chunk, step, 0)
        low_grad = lax.dot_general(hid[...], aup_ref[...], nt, preferred_element_type=f32)
        low_grad_t = low_grad.T.astype(bf16)
        low_t = low_v[r].astype(f32).T.astype(bf16)
        up_part = jnp.dot(low_t, hid[...], preferred_element_type=f32)
        down_part = jnp.dot(
            low_grad_t, xs[r, :, :, :width].reshape(2 * rows, width), preferred_element_type=f32
        )
        if r == 0:
            gb_ref[...] = up_part
            gat_ref[...] = down_part
        else:
            gb_ref[...] += up_part
            gat_ref[...] += down_part

    def combine(r):
        pair[r].wait()
        part[r, core] = (part[r, core].astype(f32) + twin_in[r].astype(f32)).astype(bf16)
        if r:
            back[r - 1].start()

    scatter = [
        remote(scat_out.at[peer], scat_in.at[j], sc_send.at[j], sc_recv.at[j], peer, "dp")
        for j, peer in enumerate(others, 1)
    ]
    collect = [
        remote(whole.at[dp], whole.at[dp], ga_send.at[j], ga_recv.at[j], peer, "dp")
        for j, peer in enumerate(others, 1)
    ]
    share_out = [
        remote(share_in.at[dp], share_in.at[dp], sh_send.at[j], sh_recv.at[j], peer, "dp")
        for j, peer in enumerate(others, 1)
    ]
    hops = [
        remote(share_hop.at[2 * n], share_hop.at[2 * n + 1], hop_send.at[n], hop_recv.at[n], dev)
        for n, dev in enumerate((twin, x_dev, y_dev))
    ]
    mix = lambda ref, i, a, c: ref[(i * kron_n + a) * kron_n + c]

    def expand_adapters():
        aup_ref[...] = jnp.zeros_like(aup_ref)
        for e in range(2):
            for a in range(kron_n):
                for c in range(kron_n):
                    block = sum(mix(sd_ref, i, a, c) * fd_ref[e, i] for i in range(kron_n))
                    adt_ref[
                        e * rank + c * cols_d : e * rank + (c + 1) * cols_d,
                        a * rows_d : (a + 1) * rows_d,
                    ] = block.astype(bf16)
                strip = [
                    sum(mix(su_ref, i, a, c) * fu_ref[e, i] for i in range(kron_n))
                    for c in range(kron_n)
                ]
                aup_ref[
                    e * rank + a * rows_u : e * rank + (a + 1) * rows_u, e * ff : (e + 1) * ff
                ] = jnp.concatenate(strip, axis=1).astype(bf16)

    def fold(product):
        half = product[:8]
        for at in range(8, product.shape[0], 8):
            half = half + product[at : at + 8]
        full = half.shape[1] // 128 * 128
        out = half[:, :128]
        for at in range(128, full, 128):
            out = out + half[:, at : at + 128]
        if full < half.shape[1]:
            rest = half.shape[1] - full
            pad = jnp.zeros((8, 128 - rest), f32)
            out = out + jnp.concatenate([half[:, full:], pad], axis=1)
        return out

    def contract():
        down_at = lambda e, a, c: gat_ref[
            e * rank + c * cols_d : e * rank + (c + 1) * cols_d, a * rows_d : (a + 1) * rows_d
        ]
        up_at = lambda e, a, c: gb_ref[
            e * rank + a * rows_u : e * rank + (a + 1) * rows_u,
            e * ff + c * cols_u : e * ff + (c + 1) * cols_u,
        ]
        sides = ((sd_ref, fd_ref, down_at, 0, rows_d), (su_ref, fu_ref, up_at, rows_d, cols_u))
        for side, (mixer, factor, block_at, start, wide) in enumerate(sides):
            tall = factor.shape[2]
            for e in range(2):
                totals = [None] * kron_n
                for a in range(kron_n):
                    for c in range(kron_n):
                        block = block_at(e, a, c)
                        for i in range(kron_n):
                            term = mix(mixer, i, a, c) * block
                            totals[i] = term if totals[i] is None else totals[i] + term
                            place = ((side * kron_n + i) * kron_n + a) * kron_n + c
                            piece = fold(factor[e, i] * block)
                            if e:
                                piece = piece + share_parts[place]
                            share_parts[place] = piece
                for i in range(kron_n):
                    top = (e * kron_n + i) * tall
                    terms[top : top + tall, start : start + wide] = totals[i]
        flat = jnp.sum(share_parts[...], axis=1)
        share_in[dp] = jnp.broadcast_to(jnp.sum(flat.T, axis=0, keepdims=True), (8, 128))

    for n in (4, 5, 0):
        tok[n].start()
    expand_adapters()
    for load in loads[:2]:
        load.wait()
    tok[0].wait_recv()
    loads[2].wait()
    forward(0)
    pair[0].start()
    tok[4].wait_recv()
    tok[6].start()
    tok[1].start()
    tok[5].wait_recv()
    tok[7].start()
    tok[2].start()
    for n in (5, 4, 0):
        grd[n].start()
    tok[1].wait_recv()
    forward(1)
    pair[1].start()
    tok[6].wait_recv()
    tok[7].wait_recv()
    tok[3].start()
    tok[2].wait_recv()
    forward(2)
    pair[2].start()
    grd[5].wait_recv()
    grd[7].start()
    grd[2].start()
    grd[4].wait_recv()
    grd[6].start()
    grd[1].start()
    combine(1)
    tok[3].wait_recv()
    forward(3)
    pair[3].start()
    combine(2)
    grd[0].wait_recv()
    backward(0)
    combine(3)
    combine(0)
    grd[6].wait_recv()
    grd[7].wait_recv()
    grd[3].start()
    grd[1].wait_recv()
    backward(1)
    grd[2].wait_recv()
    backward(2)
    grd[3].wait_recv()
    backward(3)

    terms[:, rows_d:] = jnp.zeros_like(terms[:, rows_d:])
    contract()
    scat_out[...] = terms[...].astype(bf16).reshape(scat_out.shape)
    for copy in scatter + share_out:
        copy.start()
    total = part[0, core].astype(f32)
    for n in range(3):
        back[n].wait()
        total = total + mixed_in[n + 1].astype(f32)
    mixed_ref[...] = total.astype(bf16)
    span = terms.shape[0] // n_dp
    own = terms[pl.ds(pl.multiple_of(dp * span, span), span), :]
    for j, copy in enumerate(scatter, 1):
        copy.wait()
        own = own + scat_in[j].astype(f32)
    whole[dp] = own.astype(bf16)
    for copy in collect:
        copy.start()
    for copy in share_out:
        copy.wait()
    share = share_in[0]
    for j in range(1, n_dp):
        share = share + share_in[j]
    for n, copy in enumerate(hops):
        share_hop[2 * n] = share
        copy.start()
        copy.wait()
        share = share + share_hop[2 * n + 1]
    share_ref[...] = share
    for copy in collect:
        copy.wait()
    result = whole[...].reshape(terms.shape).astype(f32)
    fdown_ref[...] = result[:, :rows_d]
    fup_ref[...] = result[:, rows_d : rows_d + cols_u]
    for copy in tok + grd:
        copy.wait_send()


def fused_device(
    tokens, grad_mixed, expert_ids, gate_probs, gate_proj, up_proj, down_proj,
    share_down, share_up, factor_down, factor_up,
):
    f32, bf16 = jnp.float32, jnp.bfloat16
    rows, width = tokens.shape
    members, ff = gate_proj.shape[0], gate_proj.shape[2]
    kron_n, rows_d, cols_d = factor_down.shape[1:]
    rows_u, cols_u = factor_up.shape[2:]
    rank = kron_n * cols_d
    n_dp = lax.axis_size("dp")
    terms = members * kron_n * cols_d
    padded = rows_d + (cols_u + 127) // 128 * 128
    vmem = pl.BlockSpec(memory_space=pltpu.VMEM)
    smem = pl.BlockSpec(memory_space=pltpu.SMEM)
    hbm = pl.BlockSpec(memory_space=pl.ANY)
    dma = pltpu.SemaphoreType.DMA
    pairs = members * 4 * 2 * rows
    mixed, fdown, fup, share = pl.pallas_call(
        group_kernel,
        out_shape=(
            jax.ShapeDtypeStruct((rows, width), bf16),
            jax.ShapeDtypeStruct((terms, rows_d), f32),
            jax.ShapeDtypeStruct((terms, cols_u), f32),
            jax.ShapeDtypeStruct((8, 128), f32),
        ),
        in_specs=[smem] * 2 + [vmem] * 6 + [hbm] * 3,
        out_specs=(vmem, vmem, vmem, vmem),
        scratch_shapes=[
            pltpu.VMEM((members * rank, width), bf16),
            pltpu.VMEM((members * rank, members * ff), bf16),
            pltpu.VMEM((members * rank, width), f32),
            pltpu.VMEM((members * rank, members * ff), f32),
            pltpu.VMEM((terms, padded), f32),
            pltpu.VMEM((2 * kron_n**3, 8, 128), f32),
            pltpu.VMEM((n_dp, 8, 128), f32),
            pltpu.VMEM((6, 8, 128), f32),
            pltpu.VMEM((n_dp, terms // n_dp, padded), bf16),
            pltpu.VMEM((n_dp, terms // n_dp, padded), bf16),
            pltpu.VMEM((n_dp, terms // n_dp, padded), bf16),
            pltpu.VMEM((4, 2, rows, width + 128), bf16),
            pltpu.VMEM((4, 2, rows, width), bf16),
            pltpu.VMEM((members, width, ff), bf16),
            pltpu.VMEM((members, width, ff), bf16),
            pltpu.VMEM((members * ff, width), bf16),
            pltpu.VMEM((4, 2 * rows, members * ff), f32),
            pltpu.VMEM((4, 2 * rows, members * rank), bf16),
            pltpu.VMEM((2 * rows, members * ff), bf16),
            pltpu.VMEM((4, 2, rows, width), bf16),
            pltpu.VMEM((4, rows, width), bf16),
            pltpu.VMEM((4, rows, width), bf16),
            dma((3,)), dma((8,)), dma((8,)), dma((8,)), dma((8,)),
            dma((4,)), dma((4,)), dma((4,)), dma((4,)),
            dma((n_dp,)), dma((n_dp,)), dma((n_dp,)), dma((n_dp,)),
            dma((n_dp,)), dma((n_dp,)), dma((3,)), dma((3,)),
        ],
        compiler_params=pltpu.CompilerParams(
            collective_id=0, has_side_effects=True, vmem_limit_bytes=58 * 1024 * 1024
        ),
        cost_estimate=pl.CostEstimate(
            flops=8 * pairs * width * ff, bytes_accessed=6 * members * width * ff,
            transcendentals=pairs * ff,
        ),
    )(
        share_down.reshape(-1), share_up.reshape(-1), tokens, grad_mixed,
        expert_ids.T, gate_probs.T, jnp.swapaxes(factor_down, 2, 3), factor_up,
        gate_proj, up_proj, down_proj.reshape(members * ff, width),
    )
    fdown = jnp.swapaxes(fdown.reshape(members, kron_n, cols_d, rows_d), 2, 3)
    fup = fup.reshape(factor_up.shape)
    share = share[0].reshape((2,) + share_down.shape)
    return (mixed, fdown, fup, share[0], share[1])


def solution(mesh):
    body = fused_device if mesh.shape["expert"] == 8 else on_device
    return jax.shard_map(
        body,
        mesh=mesh,
        in_specs=(
            P(("dp", "expert"), None),
            P(("dp", "expert"), None),
            P(("dp", "expert"), None),
            P(("dp", "expert"), None),
            P("expert", None, None),
            P("expert", None, None),
            P("expert", None, None),
            P(),
            P(),
            P("expert", None, None, None),
            P("expert", None, None, None),
        ),
        out_specs=(
            P(("dp", "expert"), None),
            P("expert", None, None, None),
            P("expert", None, None, None),
            P(),
            P(),
        ),
        check_vma=False,
    )
```
